128 devices in a mesh: rows: 16 (over x, z), slab: 8 (over y, core).
Axes of the slice: x: 4, y: 4, z: 4, core: 2. Of those that a mesh axis runs over, the one named last changes fastest.
Arguments:
- coefficients: bfloat16 [49152, 1024], P('rows', 'slab'), may hold values from -1.1953125 to 1.1953125
- occupations: bfloat16 [1, 1024], P(None, 'slab'), may hold values from 0.049804688 to 2
- energies: bfloat16 [1, 1024], P(None, 'slab'), may hold values from -2 to 1
- send_lists: int32 [16, 16, 2], P('rows'), may hold values from 0 to 23, as said below
- pair_rows: int32 [6144], P(('rows', 'slab')), may hold values from 0 to 2
- pair_sources: int32 [6144], P(('rows', 'slab')), may hold values from 0 to 55
Outputs:
- density: float32 [6144, 128, 128], P(('rows', 'slab'))
- energy_density: float32 [6144, 128, 128], P(('rows', 'slab'))
The draws below stay inside these ranges and needn't reach their ends.
Inputs may be any that keep to these rules, and one draw needn't show every extreme that they name: Each send_lists[p, r] names 2 different local row blocks of the sender p.
All inputs are finite; a program needn't handle non-finite values.
Results may differ from the reference program's by a relative error of at most 0.0028.
Values may be sent and summed in bfloat16 or wider, within the bound.
No kernel may reach another device: no remote copies, remote signals or barrier semaphores. Data moves between devices by JAX's collectives and lax.ppermute only.
A program may use at most 128 MiB of HBM per device.

```python
import jax
import jax.numpy as jnp
from jax import lax

BS = 128
KCOLS = 1024
BLK_DEV = 24
SEND_CAP = 2
PAIRS_DEV = 48
ORBITALS = 49152
PAIRS = 6144
SOURCES = 56
N_ROWS = 16
N_SLAB = 8


def draw_send_lists(key, part):
    key = jax.random.fold_in(key, 5)
    scores = jax.random.randint(key, (N_ROWS, N_ROWS, BLK_DEV), 0, 1 << 20)
    scores = scores * BLK_DEV + jnp.arange(BLK_DEV, dtype=jnp.int32)
    order = jnp.argsort(scores, axis=-1)
    return order[..., :SEND_CAP].astype(jnp.int32)


def touch_ends(entries, rng, least, largest):
    longest = entries.shape.index(max(entries.shape))
    spots = []
    for shift in (0, 1):
        where = [jax.random.randint(jax.random.fold_in(rng, axis), (), 0, length) for axis, length in enumerate(entries.shape)]
        where[longest] = (where[longest] + shift) % entries.shape[longest]
        spots.append(tuple(where))
    return entries.at[spots[0]].set(least).at[spots[1]].set(largest)


def levels(own_key, dims, split, low, top_value):
    gain, own = 1.0, jax.random.fold_in(own_key, 6)
    for dim, shards_of in split:
        heights = jnp.exp(jax.random.uniform(jax.random.fold_in(own, dim), (shards_of,), jnp.float32, low / len(split), top_value / len(split)))
        gain = gain * jnp.repeat(heights, dims[dim] // shards_of).reshape([-1 if axis == dim else 1 for axis in range(len(dims))])
    return gain


def scatter_about(key, dims, scale, most, cuts=(), held_as=jnp.bfloat16):
    factor_of = levels(key, dims, cuts, -0.22, 0.18) if cuts else 1.0
    entries = jax.random.normal(key, dims, jnp.float32) * scale * factor_of
    return jnp.minimum(jnp.maximum(entries, -most), most).astype(held_as)


def setup_inputs(seed: int = 0) -> dict:
    key_list = jax.random.split(jax.random.key(seed), 7)
    coefficients = scatter_about(key_list[0], (ORBITALS, KCOLS), 0.18, 1.1953125, ((0, 16), (1, 8)))
    occupations = jnp.clip(0.049804688 + 1.9501953 * jax.random.uniform(key_list[1], (1, KCOLS), jnp.float32) ** levels(key_list[1], (1, KCOLS), ((1, 8),), -0.2, 0.2), 0.049804688, 2.0).astype(jnp.bfloat16)
    energies = jnp.clip(-2.0 + 3.0 * jax.random.uniform(key_list[2], (1, KCOLS), jnp.float32) ** levels(key_list[2], (1, KCOLS), ((1, 8),), -0.2, 0.2), -2.0, 1.0).astype(jnp.bfloat16)
    send_lists = draw_send_lists(jax.random.fold_in(key_list[6], 71), 0)
    pair_rows = touch_ends(jax.random.randint(key_list[4], (PAIRS,), 0, BLK_DEV // N_SLAB), jax.random.fold_in(key_list[4], 1), 0, (BLK_DEV // N_SLAB) - 1).astype(jnp.int32)
    pair_sources = touch_ends(jax.random.randint(key_list[5], (PAIRS,), 0, SOURCES), jax.random.fold_in(key_list[5], 1), 0, SOURCES - 1).astype(jnp.int32)
    return dict(coefficients=coefficients, occupations=occupations, energies=energies, send_lists=send_lists, pair_rows=pair_rows, pair_sources=pair_sources)


def reference(coefficients, occupations, energies, send_lists, pair_rows, pair_sources):
    occ = occupations.astype(jnp.float32)
    level = energies.astype(jnp.float32)
    coef = coefficients.astype(jnp.float32)
    weighted = (coef * occ).astype(jnp.bfloat16)
    energetic = (coef * occ * level).astype(jnp.bfloat16)
    blocks_all = N_ROWS * BLK_DEV
    tiles = coefficients.reshape(blocks_all, BS, KCOLS)
    weight_tiles = weighted.reshape(blocks_all, BS, KCOLS)
    energy_tiles = energetic.reshape(blocks_all, BS, KCOLS)
    index = jnp.arange(PAIRS, dtype=jnp.int32)
    device = (index // PAIRS_DEV).astype(jnp.int32)
    owner = (device // N_SLAB).astype(jnp.int32)
    group = (device % N_SLAB).astype(jnp.int32)
    left = (owner * BLK_DEV + group * (BLK_DEV // N_SLAB) + pair_rows).astype(jnp.int32)
    extra = jnp.maximum(pair_sources - BLK_DEV, 0).astype(jnp.int32)
    peer = extra // SEND_CAP
    slot = extra % SEND_CAP
    remote = peer * BLK_DEV + send_lists[peer, owner, slot]
    right = jnp.where(pair_sources < BLK_DEV, owner * BLK_DEV + pair_sources, remote).astype(jnp.int32)
    left_groups = left.reshape(-1, 8)
    right_groups = right.reshape(-1, 8)

    def one_group(pieces):
        lidx, ridx = pieces
        other = tiles[ridx].astype(jnp.float32)
        dens = jnp.einsum('pak,pbk->pab', weight_tiles[lidx].astype(jnp.float32), other)
        edens = jnp.einsum('pak,pbk->pab', energy_tiles[lidx].astype(jnp.float32), other)
        return dens, edens

    dens, edens = lax.map(one_group, (left_groups, right_groups))
    return dens.reshape(PAIRS, BS, BS), edens.reshape(PAIRS, BS, BS)
```

```python
import functools

import jax
import jax.numpy as jnp
from jax import lax
from jax.experimental import pallas as pl
from jax.experimental.pallas import tpu as pltpu
from jax.sharding import PartitionSpec as P

BS = 128
YS = 4
UNROLL = 4
VM = pl.BlockSpec(memory_space=pltpu.VMEM)
SM = pl.BlockSpec(memory_space=pltpu.SMEM)
ANY = pl.BlockSpec(memory_space=pl.ANY)


def load_all(held, s_ref, sem):
    copies = [pltpu.make_async_copy(ref, s_ref.at[k], sem.at[k]) for k, ref in enumerate(held)]
    for copy in copies:
        copy.start()
    return copies


def list_pairs(wanted, order, pairs):
    def add(g, count):
        order[count] = g
        return count + wanted(g).astype(jnp.int32)

    return lax.fori_loop(0, pairs, add, 0)


def run_pairs(order, count, row_ref, block_of, s_ref, w_ref, outs, stage, sem):
    def copies(j):
        return [pltpu.make_async_copy(stage.at[n, j], outs[n].at[order[j]], sem.at[n, j]) for n in range(2)]

    def compute(t, _):
        for u in range(UNROLL):
            j = t * UNROLL + u
            g = order[jnp.minimum(j, count - 1)]
            first = pl.multiple_of(block_of(g) * BS, BS)
            other = jnp.concatenate([s_ref[k, pl.ds(first, BS), :] for k in range(s_ref.shape[0])], axis=1)
            both = lax.dot_general(
                w_ref[row_ref[g]], other, (((1,), (1,)), ((), ())), preferred_element_type=jnp.float32
            )
            stage[0, j] = both[:BS]
            stage[1, j] = both[BS:]
        for u in range(UNROLL):
            j = t * UNROLL + u

            @pl.when(j < count)
            def _():
                for copy in copies(j):
                    copy.start()

        return 0

    def drain(j, _):
        for copy in copies(j):
            copy.wait()
        return 0

    lax.fori_loop(0, (count + UNROLL - 1) // UNROLL, compute, 0)
    lax.fori_loop(0, count, drain, 0)


def near_kernel(row_ref, src_ref, q_ref, level_ref, *refs, group, blocks):
    held = refs[:8]
    dens_ref, ener_ref, w_ref, token_ref, s_ref, stage, order, in_sem, sem = refs[8:]
    loads = load_all(held, s_ref, in_sem)
    count = list_pairs(lambda g: src_ref[g] < blocks, order, row_ref.shape[0])
    q = q_ref[0]
    c = q % 2
    for s in range(8):
        mine = s < 4
        core = c if mine else 1 - c
        turn = (0, 1 + core, 2 - core, 3)[s % 4]
        occ = level_ref[turn, 0 if mine else 2]
        level = level_ref[turn, 1 if mine else 3]
        loads[s].wait()
        for i in range(group):
            first = pl.multiple_of((q * group + i) * BS, BS)
            weighted = s_ref[s, pl.ds(first, BS), :].astype(jnp.float32) * occ
            w_ref[i, :BS, s * BS : (s + 1) * BS] = weighted.astype(jnp.bfloat16)
            w_ref[i, BS:, s * BS : (s + 1) * BS] = (weighted * level).astype(jnp.bfloat16)
    run_pairs(order, count, row_ref, lambda g: src_ref[g], s_ref, w_ref, [dens_ref, ener_ref], stage, sem)
    token_ref[...] = jnp.zeros_like(token_ref)


def far_kernel(row_ref, src_ref, w_ref, dens_in, ener_in, *refs, blocks):
    held = refs[:8]
    dens_ref, ener_ref, s_ref, stage, order, in_sem, sem = refs[8:]
    loads = load_all(held, s_ref, in_sem)
    count = list_pairs(lambda g: src_ref[g] >= blocks, order, row_ref.shape[0])
    for load in loads:
        load.wait()
    run_pairs(order, count, row_ref, lambda g: src_ref[g] - blocks, s_ref, w_ref, [dens_ref, ener_ref], stage, sem)


def hop(x, step):
    pairs = [(2 * y + c, 2 * ((y + YS + step * (1 - 2 * c)) % YS) + c) for y in range(YS) for c in range(2)]
    return lax.ppermute(x, "slab", pairs)


def turn(x, dy):
    pairs = [(2 * y + c, 2 * ((y + dy) % YS) + c) for y in range(YS) for c in range(2)]
    return lax.ppermute(x, "slab", pairs)


def swap(x):
    return lax.ppermute(x, "slab", [(q, q ^ 1) for q in range(2 * YS)])


def exchange(tiles, picks):
    picked = tiles.reshape(-1, BS, BS)[picks]
    return lax.all_to_all(picked, "rows", split_axis=0, concat_axis=0, tiled=True).reshape(-1, BS)


def after(x, *others):
    return lax.optimization_barrier((x, *others))[0]


def body(coefficients, occupations, energies, send_lists, pair_rows, pair_sources):
    blocks = coefficients.shape[0] // BS
    shards = lax.axis_size("slab")
    group = blocks // shards
    pairs = pair_rows.shape[0]
    own = coefficients
    front, back = hop(own, 1), hop(own, -1)
    level = jnp.concatenate([occupations, energies], axis=0)
    level = jnp.concatenate([level, swap(level)], axis=0)
    got = exchange(own, after(send_lists[0], level))
    levels = jnp.stack([level, turn(level, 1), turn(level, -1), turn(level, 2)])
    last = hop(after(front, back, levels), 1)
    levels = levels.astype(jnp.float32)[:, :, None, :]
    got_front, got_back = hop(got, 1), hop(got, -1)
    got_last = exchange(last, send_lists[0])
    held = [own, front, back, last]
    held = held + [swap(x) for x in held]
    q = lax.axis_index("slab").reshape(1).astype(jnp.int32)

    out = jax.ShapeDtypeStruct((pairs, BS, BS), jnp.float32)
    slots = pairs + UNROLL

    def scratch(rows):
        return [
            pltpu.VMEM((shards, rows, BS), jnp.bfloat16),
            pltpu.VMEM((2, slots, BS, BS), jnp.float32),
            pltpu.SMEM((slots,), jnp.int32),
            pltpu.SemaphoreType.DMA((shards,)),
            pltpu.SemaphoreType.DMA((2, slots)),
        ]

    params = pltpu.CompilerParams(vmem_limit_bytes=24 * 1024 * 1024)
    cost = pl.CostEstimate(flops=pairs * 4 * BS * BS * shards * BS, bytes_accessed=12 << 20, transcendentals=0)
    dens, ener, weights, token = pl.pallas_call(
        functools.partial(near_kernel, group=group, blocks=blocks),
        in_specs=[SM, SM, SM, VM] + [ANY] * len(held),
        out_specs=[ANY, ANY, VM, VM],
        scratch_shapes=scratch(blocks * BS),
        out_shape=[
            out,
            out,
            jax.ShapeDtypeStruct((group, 2 * BS, shards * BS), jnp.bfloat16),
            jax.ShapeDtypeStruct((8, BS), jnp.float32),
        ],
        compiler_params=params,
        cost_estimate=cost,
    )(pair_rows, pair_sources, q, levels, *held)
    received = [got, after(got_front, token), after(got_back, token), got_last]
    received = received + [swap(x) for x in received]
    return pl.pallas_call(
        functools.partial(far_kernel, blocks=blocks),
        in_specs=[SM, SM, VM, ANY, ANY] + [ANY] * len(received),
        out_specs=[ANY, ANY],
        scratch_shapes=scratch(got.shape[0]),
        out_shape=[out, out],
        input_output_aliases={3: 0, 4: 1},
        compiler_params=params,
        cost_estimate=cost,
    )(pair_rows, pair_sources, weights, dens, ener, *received)


def solution(mesh):
    placed = (
        P("rows", "slab"),
        P(None, "slab"),
        P(None, "slab"),
        P("rows", None, None),
        P(("rows", "slab")),
        P(("rows", "slab")),
    )
    return jax.shard_map(
        body,
        mesh=mesh,
        in_specs=placed,
        out_specs=(P(("rows", "slab"), None, None), P(("rows", "slab"), None, None)),
        check_vma=False,
    )
```

```python
import functools

import jax
import jax.numpy as jnp
from jax import lax
from jax.experimental import pallas as pl
from jax.experimental.pallas import tpu as pltpu
from jax.sharding import PartitionSpec as P

BS = 128
YS = 4
UNROLL = 3
PART = 16
VM = pl.BlockSpec(memory_space=pltpu.VMEM)
SM = pl.BlockSpec(memory_space=pltpu.SMEM)
HB = pl.BlockSpec(memory_space=pltpu.HBM)
ANY = pl.BlockSpec(memory_space=pl.ANY)


def load_all(held, s_ref, sem):
    copies = [pltpu.make_async_copy(ref, s_ref.at[k], sem.at[k]) for k, ref in enumerate(held)]
    for copy in copies:
        copy.start()
    return copies


def list_pairs(bucket, pairs, order, counts):
    span = order.shape[0] // counts.shape[0]
    for n in range(counts.shape[0]):
        counts[n] = 0

    def add(g, _):
        n = bucket(g)
        at = counts[n]
        order[n * span + at] = g
        counts[n] = at + 1
        return 0

    lax.fori_loop(0, pairs, add, 0)


def list_batches(buckets, group, order, counts, batch, total):
    span = order.shape[0] // counts.shape[0]
    for n in buckets:

        def put(t, total, n=n):
            batch[3 * total] = n % group
            batch[3 * total + 1] = order[n * span + 2 * t]
            batch[3 * total + 2] = jnp.where(2 * t + 1 < counts[n], order[n * span + 2 * t + 1], -1)
            return total + 1

        total = lax.fori_loop(0, (counts[n] + 1) // 2, put, total)
    return total


def out_copies(b, batch, outs, stage, sem, act):
    def both(j, g):
        for n in range(2):
            act(pltpu.make_async_copy(stage.at[n, j], outs[n].at[g], sem.at[n, j]))

    both(2 * b, batch[3 * b + 1])
    second = batch[3 * b + 2]

    @pl.when(second >= 0)
    def _():
        both(2 * b + 1, second)


def run_batches(start, stop, batch, tiles, w_ref, outs, stage, sem):
    def compute(t, _):
        for u in range(UNROLL):
            b = jnp.minimum(start + t * UNROLL + u, stop - 1)
            first, second = batch[3 * b + 1], batch[3 * b + 2]
            other = jnp.concatenate([tiles(first), tiles(jnp.where(second < 0, first, second))], axis=0)
            both = lax.dot_general(
                w_ref[batch[3 * b]], other, (((1,), (1,)), ((), ())), preferred_element_type=jnp.float32
            )
            j = 2 * (start + t * UNROLL + u)
            for n in range(2):
                stage[n, j] = both[n * BS : (n + 1) * BS, :BS]
                stage[n, j + 1] = both[n * BS : (n + 1) * BS, BS:]
        for u in range(UNROLL):
            b = start + t * UNROLL + u

            @pl.when(b < stop)
            def _():
                out_copies(b, batch, outs, stage, sem, lambda copy: copy.start())

        return 0

    lax.fori_loop(0, (stop - start + UNROLL - 1) // UNROLL, compute, 0)


def drain(total, batch, outs, stage, sem):
    def one(b, _):
        out_copies(b, batch, outs, stage, sem, lambda copy: copy.wait())
        return 0

    lax.fori_loop(0, total, one, 0)


def block_tiles(s_ref, first):
    return jnp.concatenate([s_ref[k, pl.ds(first, BS), :] for k in range(s_ref.shape[0])], axis=1)


def near_kernel(row_ref, src_ref, q_ref, level_ref, *refs, group, blocks):
    held = refs[:8]
    dens_ref, ener_ref, w_ref, far_batch, far_total, s_ref, stage, order, counts, batch, in_sem, sem = refs[8:]
    loads = load_all(held, s_ref, in_sem)
    pairs, half = row_ref.shape[0], counts.shape[0] // group - 1

    def bucket(g):
        kind = jnp.where(src_ref[g] < blocks, 0, 1 + (src_ref[g] - blocks) // PART)
        return kind * group + row_ref[g]

    list_pairs(bucket, pairs, order, counts)
    zero = jnp.int32(0)
    total = list_batches(range(group), group, order, counts, batch, zero)
    done = zero
    for n in range(half):
        done = list_batches(range((n + 1) * group, (n + 2) * group), group, order, counts, far_batch, done)
        far_total[n] = done
    c = q_ref[0] % 2
    for s in range(8):
        mine = s < 4
        core = c if mine else 1 - c
        turn = (0, 1 + core, 2 - core, 3)[s % 4]
        occ = level_ref[turn, 0 if mine else 2]
        level = level_ref[turn, 1 if mine else 3]
        loads[s].wait()
        for i in range(group):
            first = pl.multiple_of((q_ref[0] * group + i) * BS, BS)
            weighted = s_ref[s, pl.ds(first, BS), :].astype(jnp.float32) * occ
            w_ref[i, :BS, s * BS : (s + 1) * BS] = weighted.astype(jnp.bfloat16)
            w_ref[i, BS:, s * BS : (s + 1) * BS] = (weighted * level).astype(jnp.bfloat16)

    def tiles(g):
        return block_tiles(s_ref, pl.multiple_of(src_ref[g] * BS, BS))

    outs = [dens_ref, ener_ref]
    run_batches(zero, total, batch, tiles, w_ref, outs, stage, sem)
    drain(total, batch, outs, stage, sem)


def far_kernel(src_ref, batch, totals, w_ref, dens_in, ener_in, *refs, blocks):
    held = refs[:8]
    dens_ref, ener_ref, s_ref, stage, in_sem, sem = refs[8:]
    parts = totals.shape[0]
    rows = s_ref.shape[1] // parts
    loads = []
    for n in range(parts):
        part = pl.ds(n * rows, rows)
        loads.append([])
        for k, ref in enumerate(held):
            copy = pltpu.make_async_copy(ref.at[part], s_ref.at[k, part], in_sem.at[n, k])
            copy.start()
            loads[n].append(copy)

    def tiles(g):
        return block_tiles(s_ref, pl.multiple_of((src_ref[g] - blocks) * BS, BS))

    outs = [dens_ref, ener_ref]
    start = jnp.int32(0)
    for n in range(parts):
        for copy in loads[n]:
            copy.wait()
        run_batches(start, totals[n], batch, tiles, w_ref, outs, stage, sem)
        start = totals[n]
    drain(start, batch, outs, stage, sem)


def hop(x, step):
    pairs = [(2 * y + c, 2 * ((y + YS + step * (1 - 2 * c)) % YS) + c) for y in range(YS) for c in range(2)]
    return lax.ppermute(x, "slab", pairs)


def turn(x, dy):
    pairs = [(2 * y + c, 2 * ((y + dy) % YS) + c) for y in range(YS) for c in range(2)]
    return lax.ppermute(x, "slab", pairs)


def swap(x):
    return lax.ppermute(x, "slab", [(q, q ^ 1) for q in range(2 * YS)])


def exchange(tiles, picks):
    tiles = tiles.reshape(-1, BS, BS).at[picks].get(mode="promise_in_bounds", wrap_negative_indices=False)
    return lax.all_to_all(tiles, "rows", split_axis=0, concat_axis=0, tiled=True).reshape(-1, BS)


def limit(mib):
    return pltpu.CompilerParams(vmem_limit_bytes=mib * 1024 * 1024)


def hbm(x):
    return pltpu.with_memory_space_constraint(x, pltpu.HBM)


def body(coefficients, occupations, energies, send_lists, pair_rows, pair_sources):
    blocks = coefficients.shape[0] // BS
    shards = lax.axis_size("slab")
    group = blocks // shards
    pairs = pair_rows.shape[0]
    own = coefficients
    front, back = hop(own, 1), hop(own, -1)
    got = exchange(own, send_lists[0])
    level = jnp.concatenate([occupations, energies], axis=0)
    level = jnp.concatenate([level, swap(level)], axis=0)
    front, back, level, own_x = lax.optimization_barrier((front, back, level, swap(own)))
    last = hop(front, 1)
    turned = [turn(level, 1), turn(level, -1), turn(level, 2)]
    got, front, back, *turned = lax.optimization_barrier((got, front, back, *turned))
    levels = jnp.stack([level, *turned]).astype(jnp.float32)[:, :, None, :]
    got_front, got_back = hop(got, 1), hop(got, -1)
    got_last = exchange(last, send_lists[0])
    held = [own, front, back, last, own_x, swap(front), swap(back), swap(last)]
    q = lax.axis_index("slab").reshape(1).astype(jnp.int32)

    out = jax.ShapeDtypeStruct((pairs, BS, BS), jnp.float32)
    parts = got.shape[0] // (PART * BS)
    slots = pairs + 2 * (group * parts + UNROLL)
    cost = pl.CostEstimate(flops=pairs * 4 * BS * BS * shards * BS, bytes_accessed=12 << 20, transcendentals=0)
    dens, ener, weights, batch, totals = pl.pallas_call(
        functools.partial(near_kernel, group=group, blocks=blocks),
        in_specs=[SM, SM, SM, VM] + [HB] * len(held),
        out_specs=[HB, HB, VM, SM, SM],
        scratch_shapes=[
            pltpu.VMEM((shards, blocks * BS, BS), jnp.bfloat16),
            pltpu.VMEM((2, slots, BS, BS), jnp.float32),
            pltpu.SMEM(((1 + parts) * group * pairs,), jnp.int32),
            pltpu.SMEM(((1 + parts) * group,), jnp.int32),
            pltpu.SMEM((3 * slots // 2,), jnp.int32),
            pltpu.SemaphoreType.DMA((shards,)),
            pltpu.SemaphoreType.DMA((2, slots)),
        ],
        out_shape=[
            out,
            out,
            jax.ShapeDtypeStruct((group, 2 * BS, shards * BS), jnp.bfloat16),
            jax.ShapeDtypeStruct((3 * slots // 2,), jnp.int32),
            jax.ShapeDtypeStruct((parts,), jnp.int32),
        ],
        compiler_params=limit(20),
        cost_estimate=cost,
    )(pair_rows, pair_sources, q, levels, *[hbm(x) for x in held])
    got_front, got_back, weights = lax.optimization_barrier((got_front, got_back, weights))
    received = [got, got_front, got_back, got_last]
    received = received + [swap(x) for x in received]
    return pl.pallas_call(
        functools.partial(far_kernel, blocks=blocks),
        in_specs=[SM, SM, SM, VM, HB, HB] + [HB] * 7 + [ANY],
        out_specs=[HB, HB],
        scratch_shapes=[
            pltpu.VMEM((shards, got.shape[0], BS), jnp.bfloat16),
            pltpu.VMEM((2, slots, BS, BS), jnp.float32),
            pltpu.SemaphoreType.DMA((parts, shards)),
            pltpu.SemaphoreType.DMA((2, slots)),
        ],
        out_shape=[out, out],
        input_output_aliases={4: 0, 5: 1},
        compiler_params=limit(20),
        cost_estimate=cost,
    )(pair_sources, batch, totals, weights, dens, ener, *[hbm(x) for x in received[:7]], received[7])


def solution(mesh):
    placed = (
        P("rows", "slab"),
        P(None, "slab"),
        P(None, "slab"),
        P("rows", None, None),
        P(("rows", "slab")),
        P(("rows", "slab")),
    )
    return jax.shard_map(
        body,
        mesh=mesh,
        in_specs=placed,
        out_specs=(P(("rows", "slab"), None, None), P(("rows", "slab"), None, None)),
        check_vma=False,
    )
```

```python
import functools

import jax
import jax.numpy as jnp
from jax import lax
from jax.experimental import pallas as pl
from jax.experimental.pallas import tpu as pltpu
from jax.sharding import PartitionSpec as P

BS = 128
YS = 4
UNROLL = 3
PART = 16
VM = pl.BlockSpec(memory_space=pltpu.VMEM)
SM = pl.BlockSpec(memory_space=pltpu.SMEM)
HB = pl.BlockSpec(memory_space=pltpu.HBM)
ANY = pl.BlockSpec(memory_space=pl.ANY)


def load_all(held, s_ref, sem):
    copies = [pltpu.make_async_copy(ref, s_ref.at[k], sem.at[k]) for k, ref in enumerate(held)]
    for copy in copies:
        copy.start()
    return copies


def list_pairs(bucket, pairs, order, counts):
    span = order.shape[0] // counts.shape[0]
    for n in range(counts.shape[0]):
        counts[n] = 0

    def add(g, _):
        n = bucket(g)
        at = counts[n]
        order[n * span + at] = g
        counts[n] = at + 1
        return 0

    lax.fori_loop(0, pairs, add, 0)


def list_batches(buckets, group, order, counts, batch, total):
    span = order.shape[0] // counts.shape[0]
    for n in buckets:

        def put(t, total, n=n):
            batch[3 * total] = n % group
            batch[3 * total + 1] = order[n * span + 2 * t]
            batch[3 * total + 2] = jnp.where(2 * t + 1 < counts[n], order[n * span + 2 * t + 1], -1)
            return total + 1

        total = lax.fori_loop(0, (counts[n] + 1) // 2, put, total)
    return total


def out_copies(b, batch, outs, stage, sem, act):
    def both(j, g):
        for n in range(2):
            act(pltpu.make_async_copy(stage.at[n, j], outs[n].at[g], sem.at[n, j]))

    both(2 * b, batch[3 * b + 1])
    second = batch[3 * b + 2]

    @pl.when(second >= 0)
    def _():
        both(2 * b + 1, second)


def run_batches(start, stop, batch, tiles, w_ref, outs, stage, sem):
    def compute(t, _):
        for u in range(UNROLL):
            b = jnp.minimum(start + t * UNROLL + u, stop - 1)
            first, second = batch[3 * b + 1], batch[3 * b + 2]
            other = jnp.concatenate([tiles(first), tiles(jnp.where(second < 0, first, second))], axis=0)
            both = lax.dot_general(
                w_ref[batch[3 * b]], other, (((1,), (1,)), ((), ())), preferred_element_type=jnp.float32
            )
            j = 2 * (start + t * UNROLL + u)
            for n in range(2):
                stage[n, j] = both[n * BS : (n + 1) * BS, :BS]
                stage[n, j + 1] = both[n * BS : (n + 1) * BS, BS:]
        for u in range(UNROLL):
            b = start + t * UNROLL + u

            @pl.when(b < stop)
            def _():
                out_copies(b, batch, outs, stage, sem, lambda copy: copy.start())

        return 0

    lax.fori_loop(0, (stop - start + UNROLL - 1) // UNROLL, compute, 0)


def drain(total, batch, outs, stage, sem):
    def one(b, _):
        out_copies(b, batch, outs, stage, sem, lambda copy: copy.wait())
        return 0

    lax.fori_loop(0, total, one, 0)


def block_tiles(s_ref, first):
    return jnp.concatenate([s_ref[k, pl.ds(first, BS), :] for k in range(s_ref.shape[0])], axis=1)


def near_kernel(row_ref, src_ref, q_ref, level_ref, *refs, group, blocks):
    held = refs[:8]
    dens_ref, ener_ref, w_ref, far_batch, far_total, s_ref, stage, order, counts, batch, in_sem, sem = refs[8:]
    loads = load_all(held, s_ref, in_sem)
    pairs, half = row_ref.shape[0], counts.shape[0] // group - 1

    def bucket(g):
        kind = jnp.where(src_ref[g] < blocks, 0, 1 + (src_ref[g] - blocks) // PART)
        return kind * group + row_ref[g]

    list_pairs(bucket, pairs, order, counts)
    zero = jnp.int32(0)
    total = list_batches(range(group), group, order, counts, batch, zero)
    done = zero
    for n in range(half):
        done = list_batches(range((n + 1) * group, (n + 2) * group), group, order, counts, far_batch, done)
        far_total[n] = done
    for s in range(8):
        chip, row = ((0, 0), (3, 2), (1, 0), (2, 0), (0, 2), (1, 2), (3, 0), (2, 2))[s]
        occ = level_ref[chip, row]
        level = level_ref[chip, row + 1]
        loads[s].wait()
        for i in range(group):
            first = pl.multiple_of((q_ref[0] * group + i) * BS, BS)
            weighted = s_ref[s, pl.ds(first, BS), :].astype(jnp.float32) * occ
            w_ref[i, :BS, s * BS : (s + 1) * BS] = weighted.astype(jnp.bfloat16)
            w_ref[i, BS:, s * BS : (s + 1) * BS] = (weighted * level).astype(jnp.bfloat16)

    def tiles(g):
        return block_tiles(s_ref, pl.multiple_of(src_ref[g] * BS, BS))

    outs = [dens_ref, ener_ref]
    run_batches(zero, total, batch, tiles, w_ref, outs, stage, sem)
    drain(total, batch, outs, stage, sem)


def far_kernel(src_ref, batch, totals, w_ref, dens_in, ener_in, *refs, blocks):
    held = refs[:8]
    dens_ref, ener_ref, s_ref, stage, in_sem, sem = refs[8:]
    parts = totals.shape[0]
    rows = s_ref.shape[1] // parts
    loads = []
    for n in range(parts):
        part = pl.ds(n * rows, rows)
        loads.append([])
        for k, ref in enumerate(held):
            copy = pltpu.make_async_copy(ref.at[part], s_ref.at[k, part], in_sem.at[n, k])
            copy.start()
            loads[n].append(copy)

    def tiles(g):
        return block_tiles(s_ref, pl.multiple_of((src_ref[g] - blocks) * BS, BS))

    outs = [dens_ref, ener_ref]
    start = jnp.int32(0)
    for n in range(parts):
        for copy in loads[n]:
            copy.wait()
        run_batches(start, totals[n], batch, tiles, w_ref, outs, stage, sem)
        start = totals[n]
    drain(start, batch, outs, stage, sem)


def hop(x, step):
    pairs = [(2 * y + c, 2 * ((y + YS + step * (1 - 2 * c)) % YS) + c) for y in range(YS) for c in range(2)]
    return lax.ppermute(x, "slab", pairs)


def swap(x):
    return lax.ppermute(x, "slab", [(q, q ^ 1) for q in range(2 * YS)])


def exchange(tiles, picks):
    tiles = tiles.reshape(-1, BS, BS).at[picks].get(mode="promise_in_bounds", wrap_negative_indices=False)
    return lax.all_to_all(tiles, "rows", split_axis=0, concat_axis=0, tiled=True).reshape(-1, BS)


def limit(mib):
    return pltpu.CompilerParams(vmem_limit_bytes=mib * 1024 * 1024)


def hbm(x):
    return pltpu.with_memory_space_constraint(x, pltpu.HBM)


def body(coefficients, occupations, energies, send_lists, pair_rows, pair_sources):
    blocks = coefficients.shape[0] // BS
    shards = lax.axis_size("slab")
    group = blocks // shards
    pairs = pair_rows.shape[0]
    own = coefficients
    front, back = hop(own, 1), hop(own, -1)
    got = exchange(own, send_lists[0])
    level = jnp.concatenate([occupations, energies], axis=0)
    level = jnp.concatenate([level, swap(level)], axis=0)
    front, back, level, own_x = lax.optimization_barrier((front, back, level, swap(own)))
    last = hop(front, 1)
    behind = hop(level, -1)
    turned = [behind, hop(behind, -1), swap(behind)]
    got, front, back, *turned = lax.optimization_barrier((got, front, back, *turned))
    levels = jnp.stack([level, *turned]).astype(jnp.float32)[:, :, None, :]
    got_front, got_back = hop(got, 1), hop(got, -1)
    got_late, last = lax.optimization_barrier((got, last))
    got_last = exchange(last, send_lists[0])
    held = [own, front, back, last, own_x, swap(front), swap(back), swap(last)]
    q = lax.axis_index("slab").reshape(1).astype(jnp.int32)

    out = jax.ShapeDtypeStruct((pairs, BS, BS), jnp.float32)
    parts = got.shape[0] // (PART * BS)
    slots = pairs + 2 * (group * parts + UNROLL)
    cost = pl.CostEstimate(flops=1 << 10, bytes_accessed=1 << 10, transcendentals=0)
    dens, ener, weights, batch, totals = pl.pallas_call(
        functools.partial(near_kernel, group=group, blocks=blocks),
        in_specs=[SM, SM, SM, VM] + [HB] * len(held),
        out_specs=[HB, HB, VM, SM, SM],
        scratch_shapes=[
            pltpu.VMEM((shards, blocks * BS, BS), jnp.bfloat16),
            pltpu.VMEM((2, slots, BS, BS), jnp.float32),
            pltpu.SMEM(((1 + parts) * group * pairs,), jnp.int32),
            pltpu.SMEM(((1 + parts) * group,), jnp.int32),
            pltpu.SMEM((3 * slots // 2,), jnp.int32),
            pltpu.SemaphoreType.DMA((shards,)),
            pltpu.SemaphoreType.DMA((2, slots)),
        ],
        out_shape=[
            out,
            out,
            jax.ShapeDtypeStruct((group, 2 * BS, shards * BS), jnp.bfloat16),
            jax.ShapeDtypeStruct((3 * slots // 2,), jnp.int32),
            jax.ShapeDtypeStruct((parts,), jnp.int32),
        ],
        compiler_params=limit(20),
        cost_estimate=cost,
    )(pair_rows, pair_sources, q, levels, *[hbm(x) for x in held])
    got_front, got_back, weights = lax.optimization_barrier((got_front, got_back, weights))
    received = [got, got_front, got_back, got_last]
    received = received + [swap(got_late)] + [swap(x) for x in received[1:]]
    return pl.pallas_call(
        functools.partial(far_kernel, blocks=blocks),
        in_specs=[SM, SM, SM, VM, HB, HB] + [HB] * 7 + [ANY],
        out_specs=[HB, HB],
        scratch_shapes=[
            pltpu.VMEM((shards, got.shape[0], BS), jnp.bfloat16),
            pltpu.VMEM((2, slots, BS, BS), jnp.float32),
            pltpu.SemaphoreType.DMA((parts, shards)),
            pltpu.SemaphoreType.DMA((2, slots)),
        ],
        out_shape=[out, out],
        input_output_aliases={4: 0, 5: 1},
        compiler_params=limit(20),
        cost_estimate=cost,
    )(pair_sources, batch, totals, weights, dens, ener, *[hbm(x) for x in received[:7]], received[7])


def solution(mesh):
    placed = (
        P("rows", "slab"),
        P(None, "slab"),
        P(None, "slab"),
        P("rows", None, None),
        P(("rows", "slab")),
        P(("rows", "slab")),
    )
    return jax.shard_map(
        body,
        mesh=mesh,
        in_specs=placed,
        out_specs=(P(("rows", "slab"), None, None), P(("rows", "slab"), None, None)),
        check_vma=False,
    )
```

```python
import functools

import jax
import jax.numpy as jnp
from jax import lax
from jax.experimental import pallas as pl
from jax.experimental.pallas import tpu as pltpu
from jax.sharding import PartitionSpec as P

BS = 128
YS = 4
UNROLL = 3
PART = 8
VM = pl.BlockSpec(memory_space=pltpu.VMEM)
SM = pl.BlockSpec(memory_space=pltpu.SMEM)
HB = pl.BlockSpec(memory_space=pltpu.HBM)
ANY = pl.BlockSpec(memory_space=pl.ANY)


def load_all(held, s_ref, sem):
    copies = [pltpu.make_async_copy(ref, s_ref.at[k], sem.at[k]) for k, ref in enumerate(held)]
    for copy in copies:
        copy.start()
    return copies


def list_pairs(bucket, pairs, order, counts):
    span = order.shape[0] // counts.shape[0]
    for n in range(counts.shape[0]):
        counts[n] = 0

    def add(g, _):
        n = bucket(g)
        at = counts[n]
        order[n * span + at] = g
        counts[n] = at + 1
        return 0

    lax.fori_loop(0, pairs, add, 0)


def list_batches(first, parts, group, order, counts, merged, batch, totals):
    span = order.shape[0] // counts.shape[0]
    ends = []
    for i in range(group):
        end = jnp.int32(0)
        ends.append([end])
        for n in range(parts):
            bucket = first + n * group + i

            def move(t, _, bucket=bucket, end=end, i=i):
                merged[i * span + end + t] = order[bucket * span + t]
                return 0

            lax.fori_loop(0, counts[bucket], move, 0)
            end = end + counts[bucket]
            ends[i].append(end)

    total = jnp.int32(0)
    for n in range(parts):
        for i in range(group):

            def put(t, total, i=i):
                second = merged[i * span + 2 * t + 1]
                batch[3 * total] = i
                batch[3 * total + 1] = merged[i * span + 2 * t]
                batch[3 * total + 2] = jnp.where(2 * t + 1 < ends[i][parts], second, -1)
                return total + 1

            stop = (ends[i][n + 1] + (1 if n == parts - 1 else 0)) // 2
            total = lax.fori_loop(ends[i][n] // 2, stop, put, total)
        if totals is not None:
            totals[n] = total
    return total


def out_copies(b, batch, outs, stage, sem, act):
    def both(j, g):
        for n in range(2):
            act(pltpu.make_async_copy(stage.at[n, j], outs[n].at[g], sem.at[n, j]))

    both(2 * b, batch[3 * b + 1])
    second = batch[3 * b + 2]

    @pl.when(second >= 0)
    def _():
        both(2 * b + 1, second)


def run_batches(start, stop, batch, tiles, w_ref, outs, stage, sem, before=None):
    def compute(t, _):
        if before is not None:
            before(t)
        for u in range(UNROLL):
            b = jnp.minimum(start + t * UNROLL + u, stop - 1)
            first, second = batch[3 * b + 1], batch[3 * b + 2]
            other = jnp.concatenate([tiles(first), tiles(jnp.where(second < 0, first, second))], axis=0)
            both = lax.dot_general(
                w_ref[batch[3 * b]], other, (((1,), (1,)), ((), ())), preferred_element_type=jnp.float32
            )
            j = 2 * (start + t * UNROLL + u)
            for n in range(2):
                stage[n, j] = both[n * BS : (n + 1) * BS, :BS]
                stage[n, j + 1] = both[n * BS : (n + 1) * BS, BS:]
        for u in range(UNROLL):
            b = start + t * UNROLL + u

            @pl.when(b < stop)
            def _():
                out_copies(b, batch, outs, stage, sem, lambda copy: copy.start())

        return 0

    lax.fori_loop(0, (stop - start + UNROLL - 1) // UNROLL, compute, 0)


def drain(total, batch, outs, stage, sem):
    def one(b, _):
        out_copies(b, batch, outs, stage, sem, lambda copy: copy.wait())
        return 0

    lax.fori_loop(0, total, one, 0)


def block_tiles(s_ref, first):
    return jnp.concatenate([s_ref[k, pl.ds(first, BS), :] for k in range(s_ref.shape[0])], axis=1)


def near_kernel(row_ref, src_ref, q_ref, level_ref, *refs, group, blocks):
    held = refs[:8]
    dens_ref, ener_ref, w_ref, far_batch, far_total, s_ref, stage, order, counts, merged, batch, in_sem, sem = refs[8:]
    loads = load_all(held, s_ref, in_sem)
    pairs, half = row_ref.shape[0], counts.shape[0] // group - 1

    def bucket(g):
        kind = jnp.where(src_ref[g] < blocks, 0, 1 + (src_ref[g] - blocks) // PART)
        return kind * group + row_ref[g]

    list_pairs(bucket, pairs, order, counts)
    zero = jnp.int32(0)
    total = list_batches(0, 1, group, order, counts, merged, batch, None)
    list_batches(group, half, group, order, counts, merged, far_batch, far_total)
    for s in range(8):
        chip, row = ((0, 0), (3, 2), (1, 0), (2, 0), (0, 2), (1, 2), (3, 0), (2, 2))[s]
        occ = level_ref[chip, row]
        level = level_ref[chip, row + 1]
        loads[s].wait()
        for i in range(group):
            first = pl.multiple_of((q_ref[0] * group + i) * BS, BS)
            weighted = s_ref[s, pl.ds(first, BS), :].astype(jnp.float32) * occ
            w_ref[i, :BS, s * BS : (s + 1) * BS] = weighted.astype(jnp.bfloat16)
            w_ref[i, BS:, s * BS : (s + 1) * BS] = (weighted * level).astype(jnp.bfloat16)

    def tiles(g):
        return block_tiles(s_ref, pl.multiple_of(src_ref[g] * BS, BS))

    outs = [dens_ref, ener_ref]
    run_batches(zero, total, batch, tiles, w_ref, outs, stage, sem)
    drain(total, batch, outs, stage, sem)


def far_kernel(src_ref, batch, totals, w_ref, dens_in, ener_in, *refs, blocks):
    held = refs[:8]
    dens_ref, ener_ref, s_ref, stage, in_sem, sem = refs[8:]
    parts = totals.shape[0]
    rows = s_ref.shape[1] // parts
    loads = []
    for n in range(parts):
        part = pl.ds(n * rows, rows)
        loads.append([])
        for k, ref in enumerate(held):
            copy = pltpu.make_async_copy(ref.at[part], s_ref.at[k, part], in_sem.at[n, k])
            copy.start()
            loads[n].append(copy)

    def tiles(g):
        return block_tiles(s_ref, pl.multiple_of((src_ref[g] - blocks) * BS, BS))

    def wait(n):
        for copy in loads[n]:
            copy.wait()

    def before(t):
        for n in range(1, parts):

            @pl.when(t == totals[n - 1] // UNROLL)
            def _():
                wait(n)

    outs = [dens_ref, ener_ref]
    total = totals[parts - 1]
    wait(0)
    run_batches(jnp.int32(0), total, batch, tiles, w_ref, outs, stage, sem, before)
    for n in range(1, parts):

        @pl.when(totals[n - 1] // UNROLL >= (total + UNROLL - 1) // UNROLL)
        def _():
            wait(n)

    drain(total, batch, outs, stage, sem)


def hop(x, step):
    pairs = [(2 * y + c, 2 * ((y + YS + step * (1 - 2 * c)) % YS) + c) for y in range(YS) for c in range(2)]
    return lax.ppermute(x, "slab", pairs)


def swap(x):
    return lax.ppermute(x, "slab", [(q, q ^ 1) for q in range(2 * YS)])


def exchange(tiles, picks):
    tiles = tiles.reshape(-1, BS, BS).at[picks].get(mode="promise_in_bounds", wrap_negative_indices=False)
    return lax.all_to_all(tiles, "rows", split_axis=0, concat_axis=0, tiled=True).reshape(-1, BS)


def limit(mib):
    return pltpu.CompilerParams(vmem_limit_bytes=mib * 1024 * 1024)


def hbm(x):
    return pltpu.with_memory_space_constraint(x, pltpu.HBM)


def body(coefficients, occupations, energies, send_lists, pair_rows, pair_sources):
    blocks = coefficients.shape[0] // BS
    shards = lax.axis_size("slab")
    group = blocks // shards
    pairs = pair_rows.shape[0]
    own = coefficients
    front, back = hop(own, 1), hop(own, -1)
    got = exchange(own, send_lists[0])
    level = jnp.concatenate([occupations, energies], axis=0)
    level = jnp.concatenate([level, swap(level)], axis=0)
    front, back, level, own_x = lax.optimization_barrier((front, back, level, swap(own)))
    last = hop(front, 1)
    behind = hop(level, -1)
    turned = [behind, hop(behind, -1), swap(behind)]
    got, front, back, *turned = lax.optimization_barrier((got, front, back, *turned))
    levels = jnp.stack([level, *turned]).astype(jnp.float32)[:, :, None, :]
    got_front, got_back = hop(got, 1), hop(got, -1)
    got_late, last = lax.optimization_barrier((got, last))
    got_last = exchange(last, send_lists[0])
    held = [own, front, back, last, own_x, swap(front), swap(back), swap(last)]
    q = lax.axis_index("slab").reshape(1).astype(jnp.int32)

    out = jax.ShapeDtypeStruct((pairs, BS, BS), jnp.float32)
    parts = got.shape[0] // (PART * BS)
    slots = pairs + 2 * (group + UNROLL)
    cost = pl.CostEstimate(flops=1 << 10, bytes_accessed=1 << 10, transcendentals=0)
    dens, ener, weights, batch, totals = pl.pallas_call(
        functools.partial(near_kernel, group=group, blocks=blocks),
        in_specs=[SM, SM, SM, VM] + [HB] * len(held),
        out_specs=[HB, HB, VM, SM, SM],
        scratch_shapes=[
            pltpu.VMEM((shards, blocks * BS, BS), jnp.bfloat16),
            pltpu.VMEM((2, slots, BS, BS), jnp.float32),
            pltpu.SMEM(((1 + parts) * group * pairs,), jnp.int32),
            pltpu.SMEM(((1 + parts) * group,), jnp.int32),
            pltpu.SMEM((group * pairs + 1,), jnp.int32),
            pltpu.SMEM((3 * slots // 2,), jnp.int32),
            pltpu.SemaphoreType.DMA((shards,)),
            pltpu.SemaphoreType.DMA((2, slots)),
        ],
        out_shape=[
            out,
            out,
            jax.ShapeDtypeStruct((group, 2 * BS, shards * BS), jnp.bfloat16),
            jax.ShapeDtypeStruct((3 * slots // 2,), jnp.int32),
            jax.ShapeDtypeStruct((parts,), jnp.int32),
        ],
        compiler_params=limit(20),
        cost_estimate=cost,
    )(pair_rows, pair_sources, q, levels, *[hbm(x) for x in held])
    got_front, got_back, weights = lax.optimization_barrier((got_front, got_back, weights))
    received = [got, got_front, got_back, got_last]
    received = received + [swap(got_late)] + [swap(x) for x in received[1:]]
    return pl.pallas_call(
        functools.partial(far_kernel, blocks=blocks),
        in_specs=[SM, SM, SM, VM, HB, HB] + [HB] * 7 + [ANY],
        out_specs=[HB, HB],
        scratch_shapes=[
            pltpu.VMEM((shards, got.shape[0], BS), jnp.bfloat16),
            pltpu.VMEM((2, slots, BS, BS), jnp.float32),
            pltpu.SemaphoreType.DMA((parts, shards)),
            pltpu.SemaphoreType.DMA((2, slots)),
        ],
        out_shape=[out, out],
        input_output_aliases={4: 0, 5: 1},
        compiler_params=limit(20),
        cost_estimate=cost,
    )(pair_sources, batch, totals, weights, dens, ener, *[hbm(x) for x in received[:7]], received[7])


def solution(mesh):
    placed = (
        P("rows", "slab"),
        P(None, "slab"),
        P(None, "slab"),
        P("rows", None, None),
        P(("rows", "slab")),
        P(("rows", "slab")),
    )
    return jax.shard_map(
        body,
        mesh=mesh,
        in_specs=placed,
        out_specs=(P(("rows", "slab"), None, None), P(("rows", "slab"), None, None)),
        check_vma=False,
    )
```

```python
import functools

import jax
import jax.numpy as jnp
from jax import lax
from jax.experimental import pallas as pl
from jax.experimental.pallas import tpu as pltpu
from jax.sharding import PartitionSpec as P

BS = 128
YS = 4
UNROLL = 3
PART = 8
VM = pl.BlockSpec(memory_space=pltpu.VMEM)
SM = pl.BlockSpec(memory_space=pltpu.SMEM)
HB = pl.BlockSpec(memory_space=pltpu.HBM)
ANY = pl.BlockSpec(memory_space=pl.ANY)


def load_all(held, s_ref, sem):
    copies = [pltpu.make_async_copy(ref, s_ref.at[k], sem.at[k]) for k, ref in enumerate(held)]
    for copy in copies:
        copy.start()
    return copies


def list_pairs(bucket, pairs, order, counts):
    span = order.shape[0] // counts.shape[0]
    for n in range(counts.shape[0]):
        counts[n] = 0

    def add(g, _):
        n = bucket(g)
        at = counts[n]
        order[n * span + at] = g
        counts[n] = at + 1
        return 0

    lax.fori_loop(0, pairs, add, 0)


def list_batches(first, parts, group, order, counts, merged, batch, totals):
    span = order.shape[0] // counts.shape[0]
    ends = []
    for i in range(group):
        end = jnp.int32(0)
        ends.append([end])
        for n in range(parts):
            bucket = first + n * group + i

            def move(t, _, bucket=bucket, end=end, i=i):
                merged[i * span + end + t] = order[bucket * span + t]
                return 0

            lax.fori_loop(0, counts[bucket], move, 0)
            end = end + counts[bucket]
            ends[i].append(end)

    total = jnp.int32(0)
    for n in range(parts):
        for i in range(group):

            def put(t, total, i=i):
                second = merged[i * span + 2 * t + 1]
                batch[3 * total] = i
                batch[3 * total + 1] = merged[i * span + 2 * t]
                batch[3 * total + 2] = jnp.where(2 * t + 1 < ends[i][parts], second, -1)
                return total + 1

            stop = (ends[i][n + 1] + (1 if n == parts - 1 else 0)) // 2
            total = lax.fori_loop(ends[i][n] // 2, stop, put, total)
        if totals is not None:
            totals[n] = total
    return total


def out_copies(b, batch, outs, stage, sem, act):
    def both(j, g):
        for n in range(2):
            act(pltpu.make_async_copy(stage.at[n, j], outs[n].at[g], sem.at[n, j]))

    both(2 * b, batch[3 * b + 1])
    second = batch[3 * b + 2]

    @pl.when(second >= 0)
    def _():
        both(2 * b + 1, second)


def run_batches(start, stop, batch, tiles, w_ref, outs, stage, sem, before=None):
    def compute(t, _):
        if before is not None:
            before(t)
        for u in range(UNROLL):
            b = jnp.minimum(start + t * UNROLL + u, stop - 1)
            first, second = batch[3 * b + 1], batch[3 * b + 2]
            other = jnp.concatenate([tiles(first), tiles(jnp.where(second < 0, first, second))], axis=0)
            both = lax.dot_general(
                w_ref[batch[3 * b]], other, (((1,), (1,)), ((), ())), preferred_element_type=jnp.float32
            )
            j = 2 * (start + t * UNROLL + u)
            for n in range(2):
                stage[n, j] = both[n * BS : (n + 1) * BS, :BS]
                stage[n, j + 1] = both[n * BS : (n + 1) * BS, BS:]
        for u in range(UNROLL):
            b = start + t * UNROLL + u

            @pl.when(b < stop)
            def _():
                out_copies(b, batch, outs, stage, sem, lambda copy: copy.start())

        return 0

    lax.fori_loop(0, (stop - start + UNROLL - 1) // UNROLL, compute, 0)


def drain(total, batch, outs, stage, sem):
    def one(b, _):
        out_copies(b, batch, outs, stage, sem, lambda copy: copy.wait())
        return 0

    lax.fori_loop(0, total, one, 0)


def block_tiles(s_ref, first):
    return jnp.concatenate([s_ref[k, pl.ds(first, BS), :] for k in range(s_ref.shape[0])], axis=1)


def near_kernel(row_ref, src_ref, q_ref, level_ref, *refs, group, blocks):
    held = refs[:8]
    dens_ref, ener_ref, w_ref, far_batch, far_total, s_ref, stage, order, counts, merged, batch, in_sem, sem = refs[8:]
    loads = load_all(held, s_ref, in_sem)
    pairs, half = row_ref.shape[0], counts.shape[0] // group - 1

    def bucket(g):
        kind = jnp.where(src_ref[g] < blocks, 0, 1 + (src_ref[g] - blocks) // PART)
        return kind * group + row_ref[g]

    list_pairs(bucket, pairs, order, counts)
    zero = jnp.int32(0)
    total = list_batches(0, 1, group, order, counts, merged, batch, None)
    list_batches(group, half, group, order, counts, merged, far_batch, far_total)
    for s in range(8):
        chip, row = ((0, 0), (3, 2), (1, 0), (2, 0), (0, 2), (1, 2), (3, 0), (2, 2))[s]
        occ = level_ref[chip, row]
        level = level_ref[chip, row + 1]
        loads[s].wait()
        for i in range(group):
            first = pl.multiple_of((q_ref[0] * group + i) * BS, BS)
            weighted = s_ref[s, pl.ds(first, BS), :].astype(jnp.float32) * occ
            w_ref[i, :BS, s * BS : (s + 1) * BS] = weighted.astype(jnp.bfloat16)
            w_ref[i, BS:, s * BS : (s + 1) * BS] = (weighted * level).astype(jnp.bfloat16)

    def tiles(g):
        return block_tiles(s_ref, pl.multiple_of(src_ref[g] * BS, BS))

    outs = [dens_ref, ener_ref]
    run_batches(zero, total, batch, tiles, w_ref, outs, stage, sem)
    drain(total, batch, outs, stage, sem)


def far_kernel(src_ref, batch, totals, w_ref, dens_in, ener_in, *refs, blocks):
    held = refs[:8]
    dens_ref, ener_ref, s_ref, stage, in_sem, sem = refs[8:]
    parts = totals.shape[0]
    rows = s_ref.shape[1] // parts
    loads = []
    for n in range(parts):
        part = pl.ds(n * rows, rows)
        loads.append([])
        for k, ref in enumerate(held):
            copy = pltpu.make_async_copy(ref.at[part], s_ref.at[k, part], in_sem.at[n, k])
            copy.start()
            loads[n].append(copy)

    def tiles(g):
        return block_tiles(s_ref, pl.multiple_of((src_ref[g] - blocks) * BS, BS))

    def wait(n):
        for copy in loads[n]:
            copy.wait()

    def before(t):
        for n in range(1, parts):

            @pl.when(t == totals[n - 1] // UNROLL)
            def _():
                wait(n)

    outs = [dens_ref, ener_ref]
    total = totals[parts - 1]
    wait(0)
    run_batches(jnp.int32(0), total, batch, tiles, w_ref, outs, stage, sem, before)
    for n in range(1, parts):

        @pl.when(totals[n - 1] // UNROLL >= (total + UNROLL - 1) // UNROLL)
        def _():
            wait(n)

    drain(total, batch, outs, stage, sem)


def hop(x, step):
    pairs = [(2 * y + c, 2 * ((y + YS + step * (1 - 2 * c)) % YS) + c) for y in range(YS) for c in range(2)]
    return lax.ppermute(x, "slab", pairs)


def swap(x):
    return lax.ppermute(x, "slab", [(q, q ^ 1) for q in range(2 * YS)])


def choose(tiles, picks):
    return tiles.reshape(-1, BS, BS).at[picks].get(mode="promise_in_bounds", wrap_negative_indices=False)


def exchange(chosen):
    return lax.all_to_all(chosen, "rows", split_axis=0, concat_axis=0, tiled=True).reshape(-1, BS)


def limit(mib):
    return pltpu.CompilerParams(vmem_limit_bytes=mib * 1024 * 1024)


def hbm(x):
    return pltpu.with_memory_space_constraint(x, pltpu.HBM)


def body(coefficients, occupations, energies, send_lists, pair_rows, pair_sources):
    blocks = coefficients.shape[0] // BS
    shards = lax.axis_size("slab")
    group = blocks // shards
    pairs = pair_rows.shape[0]
    own = coefficients
    chosen = choose(own, send_lists[0])
    chosen, again = lax.optimization_barrier((chosen, own))
    front, back = hop(own, 1), hop(again, -1)
    got = exchange(chosen)
    level = jnp.concatenate([occupations, energies], axis=0)
    level = jnp.concatenate([level, swap(level)], axis=0)
    front, back, level = lax.optimization_barrier((front, back, level))
    last = hop(front, 1)
    behind = hop(level, -1)
    turned = [behind, hop(behind, -1), swap(behind)]
    got, front, back, own_x, *turned = lax.optimization_barrier((got, front, back, swap(own), *turned))
    levels = jnp.stack([level, *turned]).astype(jnp.float32)[:, :, None, :]
    got_front, got_back = hop(got, 1), hop(got, -1)
    got_late, last = lax.optimization_barrier((got, last))
    got_last = exchange(choose(last, send_lists[0]))
    held = [own, front, back, last, own_x, swap(front), swap(back), swap(last)]
    q = lax.axis_index("slab").reshape(1).astype(jnp.int32)

    out = jax.ShapeDtypeStruct((pairs, BS, BS), jnp.float32)
    parts = got.shape[0] // (PART * BS)
    slots = pairs + 2 * (group + UNROLL)
    cost = pl.CostEstimate(flops=1 << 10, bytes_accessed=1 << 10, transcendentals=0)
    dens, ener, weights, batch, totals = pl.pallas_call(
        functools.partial(near_kernel, group=group, blocks=blocks),
        in_specs=[SM, SM, SM, VM] + [HB] * len(held),
        out_specs=[HB, HB, VM, SM, SM],
        scratch_shapes=[
            pltpu.VMEM((shards, blocks * BS, BS), jnp.bfloat16),
            pltpu.VMEM((2, slots, BS, BS), jnp.float32),
            pltpu.SMEM(((1 + parts) * group * pairs,), jnp.int32),
            pltpu.SMEM(((1 + parts) * group,), jnp.int32),
            pltpu.SMEM((group * pairs + 1,), jnp.int32),
            pltpu.SMEM((3 * slots // 2,), jnp.int32),
            pltpu.SemaphoreType.DMA((shards,)),
            pltpu.SemaphoreType.DMA((2, slots)),
        ],
        out_shape=[
            out,
            out,
            jax.ShapeDtypeStruct((group, 2 * BS, shards * BS), jnp.bfloat16),
            jax.ShapeDtypeStruct((3 * slots // 2,), jnp.int32),
            jax.ShapeDtypeStruct((parts,), jnp.int32),
        ],
        compiler_params=limit(20),
        cost_estimate=cost,
    )(pair_rows, pair_sources, q, levels, *[hbm(x) for x in held])
    got_front, got_back, weights = lax.optimization_barrier((got_front, got_back, weights))
    received = [got, got_front, got_back, got_last]
    received = received + [swap(got_late)] + [swap(x) for x in received[1:]]
    return pl.pallas_call(
        functools.partial(far_kernel, blocks=blocks),
        in_specs=[SM, SM, SM, VM, HB, HB] + [HB] * 7 + [ANY],
        out_specs=[HB, HB],
        scratch_shapes=[
            pltpu.VMEM((shards, got.shape[0], BS), jnp.bfloat16),
            pltpu.VMEM((2, slots, BS, BS), jnp.float32),
            pltpu.SemaphoreType.DMA((parts, shards)),
            pltpu.SemaphoreType.DMA((2, slots)),
        ],
        out_shape=[out, out],
        input_output_aliases={4: 0, 5: 1},
        compiler_params=limit(20),
        cost_estimate=cost,
    )(pair_sources, batch, totals, weights, dens, ener, *[hbm(x) for x in received[:7]], received[7])


def solution(mesh):
    placed = (
        P("rows", "slab"),
        P(None, "slab"),
        P(None, "slab"),
        P("rows", None, None),
        P(("rows", "slab")),
        P(("rows", "slab")),
    )
    return jax.shard_map(
        body,
        mesh=mesh,
        in_specs=placed,
        out_specs=(P(("rows", "slab"), None, None), P(("rows", "slab"), None, None)),
        check_vma=False,
    )
```
